32 devices in a mesh: dp: 2 (over core), expert: 16 (over z, y, x).
Axes of the slice: x: 2, y: 2, z: 4, core: 2. Of those that a mesh axis runs over, the one named last changes fastest.
Arguments:
- tokens: bfloat16 [6144, 1024], P(('dp', 'expert')), may hold values from -6 to 6
- out_grad: bfloat16 [6144, 1024], P(('dp', 'expert')), may hold values from -2.5 to 2.5
- gates: bfloat16 [6144, 2], P(('dp', 'expert')), may hold values from 0.099609375 to 0.8984375
- expert_ids: int32 [6144, 2], P(('dp', 'expert')), may hold values from 0 to 15, all different within a row; in each aligned block of 192 rows (0 to 191, 192 to 383, ...) at most 36 rows name the same one
- w_in: bfloat16 [16, 1024, 1024], P('expert', None, 'dp'), may hold values from -0.1875 to 0.1875
- w_out: bfloat16 [16, 1024, 1024], P('expert', None, 'dp'), may hold values from -0.1875 to 0.1875
Outputs:
- d_tokens: bfloat16 [6144, 1024], P(('dp', 'expert'))
- gate_grad: bfloat16 [6144, 2], P(('dp', 'expert'))
- grad_in: float32 [16, 1024, 1024], P('expert', None, 'dp')
- grad_out: float32 [16, 1024, 1024], P('expert', None, 'dp')
The draws below stay inside these ranges and needn't reach their ends.
Inputs may be any that keep to these rules, and one draw needn't show every extreme that they name: `expert_ids`: each row names two different experts. Among the 192 rows of one device no expert is named more than 36 times, and in every draw some device names some expert exactly 36 times.
All inputs are finite; a program needn't handle non-finite values.
Results may differ from the reference program's by a relative error of at most 0.022.
Values may be sent and summed in bfloat16 or wider, within the bound.
A program may use at most 64 MiB of HBM per device.

```python
import math
import jax
import jax.numpy as jnp
import numpy as np
from jax import lax

D = 1024
FF = 1024
TOK_DEV = 192
EXPERTS = 16
CAP = 36
ROWS = 576
TOKEN_TOTAL = 6144
N_DP = 2
N_EXPERT = 16


def block_levels(own_key, dims, split, smallest, largest):
    def one(dim, blocks):
        steps = jax.random.uniform(jax.random.fold_in(jax.random.fold_in(own_key, 6), dim), (blocks,), jnp.float32, smallest / len(split), largest / len(split))
        return jnp.repeat(jnp.exp(steps), dims[dim] // blocks).reshape((-1,) + (1,) * (len(dims) - dim - 1))

    level = one(*split[0])
    for cut in split[1:]:
        level = level * one(*cut)
    return level


def shared_out(key, own, number, rows, count, top, limit, slope):
    order = jax.random.permutation(key, count)
    crowded, ordinary = load_shares(count, rows * top, limit, slope, True), load_shares(count, rows * top, limit, slope, False)
    places = jnp.arange(count)

    def named(tallies, rotation):
        used = int((tallies > 0).sum())
        fixed = max(1, used // 4)
        moved = fixed + (places - fixed + rotation * (used - fixed)) % max(1, count - fixed)
        return jnp.zeros((count,), jnp.int32).at[order[jnp.where(places < fixed, places, moved)]].set(jnp.asarray(tallies, jnp.int32))

    tallies = jnp.where(number % 4 == 0, named(crowded, number // 4), named(ordinary, number - number // 4 - 1))
    mixed = jax.random.permutation(jax.random.fold_in(own, 3), count)
    giver, sink = mixed[0:count // 2 * 2:2], mixed[1:count // 2 * 2:2]
    slack = jnp.minimum(tallies[giver] - 1, limit - tallies[sink]) // 2
    slack = jnp.where((giver == order[0]) | (sink == order[0]) | (tallies[sink] == 0), 0, jnp.maximum(slack, 0))
    moved = jax.random.randint(jax.random.fold_in(own, 4), (count // 2,), 0, 1 << 20) % (slack + 1)
    tallies = tallies.at[giver].add(-moved).at[sink].add(moved)
    members = jnp.searchsorted(jnp.cumsum(tallies), jnp.arange(rows * top), side="right").astype(jnp.int32)
    grid = members.reshape(top, rows).T
    grid = grid[jax.random.permutation(jax.random.fold_in(own, 1), rows)]
    rotation = jax.random.randint(jax.random.fold_in(own, 2), (rows, 1), 0, top)
    return jnp.take_along_axis(grid, (jnp.arange(top)[None, :] + rotation) % top, axis=1)


def load_shares(amount, total, limit, lean, full):
    portions = [(1 << 20) // math.isqrt(rank ** lean) + 1 for rank in range(1, amount + 1)]
    largest = limit if full else min(limit, max(-(-total // amount), total * portions[0] // sum(portions)))
    least = 1 if total - largest >= amount - 1 else 0
    given, spare = [largest] + [least] * (amount - 1), total - largest - least * (amount - 1)
    while spare > 0:
        movable = [i for i in range(1, amount) if given[i] < largest] or [i for i in range(1, amount) if given[i] < limit]
        mass, budget = sum([portions[i] for i in movable]), spare
        for i in movable:
            addition = min(limit - given[i], max(1, budget * portions[i] // mass), spare)
            given[i] = given[i] + addition
            spare = spare - addition
    return np.array(given)


def scatter_about(own_key, extent, deviation, limit, shards=(), kind=jnp.bfloat16):
    values = deviation * jax.random.normal(own_key, extent, jnp.float32)
    if shards:
        values = values * block_levels(own_key, extent, shards, -0.22, 0.18)
    return jnp.clip(values, -limit, limit).astype(kind)


def setup_inputs(seed: int = 0) -> dict:
    key_of = jax.random.split(jax.random.key(seed), 7)
    tokens = scatter_about(key_of[0], (TOKEN_TOTAL, D), 1.0, 6.0, ((0, 32),))
    out_grad = scatter_about(key_of[1], (TOKEN_TOTAL, D), 0.3, 2.5, ((0, 32),))
    gates = jnp.clip(0.099609375 + 0.7988281 * jax.random.uniform(key_of[2], (TOKEN_TOTAL, 2), jnp.float32) ** block_levels(key_of[2], (TOKEN_TOTAL, 2), ((0, 32),), -0.2, 0.2), 0.099609375, 0.8984375).astype(jnp.bfloat16)
    expert_ids_keys = jax.random.split(jax.random.fold_in(key_of[3], 1), TOKEN_TOTAL // TOK_DEV)
    expert_ids_turns = jax.random.permutation(jax.random.fold_in(key_of[3], 3), TOKEN_TOTAL // TOK_DEV)
    expert_ids = jax.vmap(lambda own, number: shared_out(jax.random.fold_in(key_of[3], 2), own, number, TOK_DEV, EXPERTS, 2, CAP, 0))(expert_ids_keys, expert_ids_turns).reshape((TOKEN_TOTAL, 2))
    w_in = scatter_about(key_of[4], (EXPERTS, D, FF), D ** -0.5, 0.1875, ((0, 16), (2, 2)))
    w_out = scatter_about(key_of[5], (EXPERTS, D, FF), FF ** -0.5, 0.1875, ((0, 16), (2, 2)))
    return {"tokens": tokens, "out_grad": out_grad, "gates": gates, "expert_ids": expert_ids, "w_in": w_in, "w_out": w_out}


gelu_scale = 0.7978845608028654
cubic_coef = 0.044715


def gelu_value(values):
    return 0.5 * values * (1.0 + jnp.tanh(gelu_scale * (values + cubic_coef * values * values * values)))


def gelu_slope(values):
    tanh_inner = jnp.tanh(gelu_scale * (values + cubic_coef * values * values * values))
    return 0.5 * (1.0 + tanh_inner) + 0.5 * values * (1.0 - tanh_inner * tanh_inner) * gelu_scale * (1.0 + 3.0 * cubic_coef * values * values)


def slot_positions(id_block):
    flat_ids = id_block.reshape(-1)
    onehot = (flat_ids[:, None] == jnp.arange(EXPERTS, dtype=jnp.int32)[None, :]).astype(jnp.int32)
    earlier = jnp.cumsum(onehot, axis=0) - onehot
    return (flat_ids * CAP + jnp.sum(earlier * onehot, axis=1)).astype(jnp.int32)


def reference(tokens, out_grad, gates, expert_ids, w_in, w_out):
    device_count = N_DP * N_EXPERT
    targets = jax.vmap(slot_positions)(expert_ids.reshape(device_count, TOK_DEV, 2))
    assignment = jnp.arange(2 * TOKEN_TOTAL, dtype=jnp.int32).reshape(device_count, 2 * TOK_DEV)
    device_rows = jnp.broadcast_to(jnp.arange(device_count, dtype=jnp.int32)[:, None], targets.shape)
    slot_table = jnp.full((device_count, EXPERTS * CAP), -1, jnp.int32).at[device_rows, targets].set(assignment)
    slot_table = slot_table.reshape(N_DP, N_EXPERT, EXPERTS, CAP)
    flat_gates = gates.reshape(-1)

    def one_expert(running, expert_index):
        slot_owner = lax.dynamic_index_in_dim(slot_table, expert_index, 2, False).reshape(N_DP * ROWS)
        is_filled = slot_owner >= 0
        safe_owner = jnp.maximum(slot_owner, 0).astype(jnp.int32)
        token_row = (safe_owner // 2).astype(jnp.int32)
        rows_x = jnp.where(is_filled[:, None], tokens[token_row], jnp.zeros((), jnp.bfloat16))
        rows_dy = jnp.where(is_filled[:, None], out_grad[token_row], jnp.zeros((), jnp.bfloat16))
        gate_column = jnp.where(is_filled, flat_gates[safe_owner].astype(jnp.float32), jnp.float32(0.0))[:, None]
        w_first = lax.dynamic_index_in_dim(w_in, expert_index, 0, False)
        w_second = lax.dynamic_index_in_dim(w_out, expert_index, 0, False)
        pre_act = jnp.dot(rows_x, w_first, preferred_element_type=jnp.float32)
        activated = gelu_value(pre_act).astype(jnp.bfloat16)
        dy_proj = jnp.dot(rows_dy, w_second, preferred_element_type=jnp.float32)
        d_pre = (gate_column * dy_proj * gelu_slope(pre_act)).astype(jnp.bfloat16)
        scaled = (gate_column * activated.astype(jnp.float32)).astype(jnp.bfloat16)
        dx_rows = jnp.dot(d_pre, w_first.T, preferred_element_type=jnp.float32).astype(jnp.bfloat16)
        expert_out = jnp.dot(activated, w_second.T, preferred_element_type=jnp.float32)
        gate_rows = jnp.sum(rows_dy.astype(jnp.float32) * expert_out, axis=1).astype(jnp.bfloat16)
        input_halves = rows_x.reshape(N_DP, ROWS, D).astype(jnp.float32)
        output_gradient_halves = rows_dy.reshape(N_DP, ROWS, D).astype(jnp.float32)
        preact_gradient_halves = d_pre.reshape(N_DP, ROWS, FF).astype(jnp.float32)
        scaled_halves = scaled.reshape(N_DP, ROWS, FF).astype(jnp.float32)
        leading_portion = jnp.einsum("mcu,mcs->mus", input_halves, preact_gradient_halves)
        leading_portion = lax.optimization_barrier(leading_portion.astype(jnp.bfloat16)).astype(jnp.float32)
        trailing_portion = jnp.einsum("mcu,mcs->mus", output_gradient_halves, scaled_halves)
        trailing_portion = lax.optimization_barrier(trailing_portion.astype(jnp.bfloat16)).astype(jnp.float32)
        grad_first = jnp.sum(leading_portion, axis=0)
        grad_second = jnp.sum(trailing_portion, axis=0)
        dx_total, dg_total = running
        dx_total = dx_total.at[token_row].add(jnp.where(is_filled[:, None], dx_rows.astype(jnp.float32), jnp.float32(0.0)))
        dg_total = dg_total.at[safe_owner].add(jnp.where(is_filled, gate_rows.astype(jnp.float32), jnp.float32(0.0)))
        return (dx_total, dg_total), (grad_first, grad_second)

    initial = (jnp.zeros((TOKEN_TOTAL, D), jnp.float32), jnp.zeros((2 * TOKEN_TOTAL,), jnp.float32))
    finals, stacked = lax.scan(one_expert, initial, jnp.arange(EXPERTS, dtype=jnp.int32))
    d_tokens = finals[0].astype(jnp.bfloat16)
    gate_grad = finals[1].reshape(TOKEN_TOTAL, 2).astype(jnp.bfloat16)
    return (d_tokens, gate_grad, stacked[0], stacked[1])
```

```python
import functools

import jax
import jax.numpy as jnp
from jax import lax
from jax.experimental import pallas as pl
from jax.experimental.pallas import tpu as pltpu
from jax.sharding import PartitionSpec as P

gelu_scale = 0.7978845608028654
cubic_coef = 0.044715
MESH = pl.DeviceIdType.MESH
GROUPS = 4
BF = jnp.bfloat16
F32 = jnp.float32


def paired(group, step):
    return 2 * ((group // 2 + step // 2) % 2) + (group % 2 + step % 2) % 2


def contract_first(a, b):
    return lax.dot_general(a, b, (((0,), (0,)), ((), ())), preferred_element_type=F32)


def contract_last(a, b):
    return lax.dot_general(a, b, (((1,), (1,)), ((), ())), preferred_element_type=F32)


def matmul(a, b):
    return jnp.dot(a, b, preferred_element_type=F32)


def lanes(rows, columns):
    return lax.broadcasted_iota(jnp.int32, (rows, columns), 1)


def ones_at(*conditions):
    hit = conditions[0]
    for other in conditions[1:]:
        hit = hit | other
    return jnp.where(hit, 1.0, 0.0).astype(BF)


def kernel(
    experts,
    parts,
    cap,
    chunk,
    tokens_ref,
    out_grad_ref,
    gates_ref,
    ids_ref,
    w_in_ref,
    w_out_ref,
    d_tokens_ref,
    gate_grad_ref,
    sums_in_ref,
    sums_out_ref,
    send_buf,
    recv_buf,
    ret_buf,
    back_buf,
    pick_x,
    pick_dy,
    pick_gate,
    weights_in,
    weights_out,
    rows_x,
    rows_dy,
    d_pre,
    scaled,
    part_in,
    part_out,
    send_sem,
    recv_sem,
    ret_sem,
    back_sem,
    w_send_sem,
    w_recv_sem,
    g_send_sem,
    g_recv_sem,
):
    size = experts // GROUPS
    span = size * chunk
    slots = size * cap
    tok_rows, width = tokens_ref.shape
    half = width // 2
    hidden = w_in_ref.shape[2]
    me = lax.axis_index("expert")
    my_dp = lax.axis_index("dp")
    my_group, my_member = me // size, me % size

    def expert_device(group, member):
        return {"expert": group * size + member}

    barrier = pltpu.get_barrier_semaphore()
    for step in range(GROUPS):
        for turn in range(size):
            if step or turn:
                pl.semaphore_signal(
                    barrier,
                    inc=1,
                    device_id=expert_device(paired(my_group, step), (my_member + turn) % size),
                    device_id_type=MESH,
                )
    for turn in range(1, parts):
        pl.semaphore_signal(
            barrier, inc=1, device_id={"dp": (my_dp + turn) % parts}, device_id_type=MESH
        )

    own_w = [
        pltpu.make_async_copy(w_in_ref.at[0], weights_in.at[0], w_recv_sem.at[0, 0]),
        pltpu.make_async_copy(w_out_ref.at[0], weights_out.at[0], w_recv_sem.at[1, 0]),
    ]
    for copy in own_w:
        copy.start()

    ids = ids_ref[...]
    id_0, id_1 = ids[:, 0:1], ids[:, 1:2]
    named = lanes(tok_rows, 128)
    named_0, named_1 = named == id_0, named == id_1
    later = lax.broadcasted_iota(jnp.int32, (tok_rows, tok_rows), 0) > lanes(tok_rows, tok_rows)
    earlier = matmul(ones_at(later), ones_at(named_0, named_1))
    slot_0 = jnp.sum(jnp.where(named_0, earlier, 0.0), axis=1, keepdims=True).astype(jnp.int32)
    slot_1 = jnp.sum(jnp.where(named_1, earlier, 0.0), axis=1, keepdims=True).astype(jnp.int32)
    place_0, place_1 = id_0 * chunk + slot_0, id_1 * chunk + slot_1
    line_0, line_1 = id_0 * chunk + 2 * cap, id_1 * chunk + 2 * cap
    at_slot_0, at_slot_1 = named == slot_0, named == slot_1
    gates = gates_ref[...].astype(F32)
    gate_0 = jnp.where(at_slot_0, gates[:, 0:1], 0.0).astype(BF)
    gate_1 = jnp.where(at_slot_1, gates[:, 1:2], 0.0).astype(BF)

    def selectors(group):
        lane = lanes(tok_rows, span) + group * span
        return (
            ones_at(lane == place_0, lane == place_1),
            ones_at(lane == place_0 + cap, lane == place_1 + cap),
            ones_at(lane == line_0),
            ones_at(lane == line_1),
        )

    def chunk_rows(member):
        return pl.ds(pl.multiple_of(member * chunk, 16), chunk)

    def dispatch_copy(group, member):
        return pltpu.make_async_remote_copy(
            src_ref=send_buf.at[group, chunk_rows(member)],
            dst_ref=recv_buf.at[my_group, chunk_rows(my_member)],
            send_sem=send_sem.at[group * size + member],
            recv_sem=recv_sem.at[me],
            device_id=expert_device(group, member),
            device_id_type=MESH,
        )

    def return_copy(group, member):
        return pltpu.make_async_remote_copy(
            src_ref=ret_buf.at[group, chunk_rows(member)],
            dst_ref=back_buf.at[my_group, chunk_rows(my_member)],
            send_sem=ret_sem.at[group * size + member],
            recv_sem=back_sem.at[me],
            device_id=expert_device(group, member),
            device_id_type=MESH,
        )

    def local_copy(source, target, sems):
        return pltpu.make_async_copy(
            source.at[my_group, chunk_rows(my_member)],
            target.at[my_group, chunk_rows(my_member)],
            sems.at[me],
        )

    def await_group(target, sems, group):
        for member in range(size):
            block = target.at[group, pl.ds(member * chunk, chunk)]
            pltpu.make_async_copy(block, block, sems.at[group * size + member]).wait()

    def fill(group):
        to_x, to_dy, to_line_0, to_line_1 = selectors(group)
        packed = contract_first(to_x, tokens_ref[...]) + contract_first(to_dy, out_grad_ref[...])
        line = contract_first(to_line_0, gate_0) + contract_first(to_line_1, gate_1)
        send_buf[group, :, 128:] = packed[:, 128:].astype(BF)
        send_buf[group, :, :128] = (packed[:, :128] + line).astype(BF)

    for step in (3, 2, 1, 0):
        group = paired(my_group, step)
        fill(group)
        if step == 3:
            pl.semaphore_wait(barrier, experts - 1 + parts - 1)
        for turn in range(size):
            member = (my_member + turn) % size
            if step or turn:
                dispatch_copy(group, member).start()
            else:
                local_copy(send_buf, recv_buf, recv_sem).start()
        if step == 3:
            for turn in range(1, parts):
                for n, (source, target) in enumerate(
                    ((w_in_ref, weights_in), (w_out_ref, weights_out))
                ):
                    pltpu.make_async_remote_copy(
                        src_ref=source.at[0],
                        dst_ref=target.at[parts - turn],
                        send_sem=w_send_sem.at[n, turn],
                        recv_sem=w_recv_sem.at[n, parts - turn],
                        device_id={"dp": (my_dp + turn) % parts},
                        device_id_type=MESH,
                    ).start()

    slot = lax.broadcasted_iota(jnp.int32, (slots, 1), 0)
    first = (slot // cap) * chunk
    within = slot % cap
    pick_x[...] = ones_at(lanes(slots, span) == first + within)
    pick_dy[...] = ones_at(lanes(slots, span) == first + within + cap)
    pick_gate[...] = ones_at(lanes(slots, span) == first + 2 * cap)
    at_within = lanes(slots, 128) == within

    for copy in own_w:
        copy.wait()
    for part in range(1, parts):
        for n, target in enumerate((weights_in, weights_out)):
            block = target.at[part]
            pltpu.make_async_copy(block, block, w_recv_sem.at[n, part]).wait()

    order = (0, 1, 3, 2)

    def work(turn_index, carry):
        step = turn_index + (turn_index // 2) * (5 - 2 * turn_index)
        group = paired(my_group, step)
        await_group(recv_buf, recv_sem, group)
        rows = pl.ds(pl.multiple_of(turn_index * slots, 16), slots)
        got = recv_buf[group]
        x = matmul(pick_x[...], got).astype(BF)
        dy = matmul(pick_dy[...], got).astype(BF)
        lines = matmul(pick_gate[...], got[:, :128])
        gate = jnp.sum(jnp.where(at_within, lines, 0.0), axis=1, keepdims=True)
        rows_x[rows] = x
        rows_dy[rows] = dy
        dx = None
        gate_slot = None
        for part in range(parts):
            v = matmul(x, weights_in[part])
            dy_proj = matmul(dy, weights_out[part])
            tanh_inner = jnp.tanh(gelu_scale * (v + cubic_coef * v * v * v))
            activated = (0.5 * v * (1.0 + tanh_inner)).astype(BF).astype(F32)
            slope = 0.5 * (1.0 + tanh_inner) + 0.5 * v * (
                1.0 - tanh_inner * tanh_inner
            ) * gelu_scale * (1.0 + 3.0 * cubic_coef * v * v)
            d_pre_part = (gate * dy_proj * slope).astype(BF)
            d_pre[part, rows] = d_pre_part
            scaled[part, rows] = (gate * activated).astype(BF)
            gate_part = jnp.sum(activated * dy_proj, axis=1, keepdims=True)
            dx_part = contract_last(d_pre_part, weights_in[part])
            dx = dx_part if dx is None else dx + dx_part
            gate_slot = gate_part if gate_slot is None else gate_slot + gate_part
        dx = dx.astype(BF)
        packed = contract_first(pick_x[...], dx[:, :half]) + contract_first(
            pick_dy[...], dx[:, half:]
        )
        line = contract_first(pick_gate[...], jnp.where(at_within, gate_slot, 0.0).astype(BF))
        ret_buf[group, :, 128:] = packed[:, 128:].astype(BF)
        ret_buf[group, :, :128] = (packed[:, :128] + line).astype(BF)

        for turn in range(1, size):
            return_copy(group, (my_member + turn) % size).start()

        @pl.when(turn_index == 0)
        def _():
            local_copy(ret_buf, back_buf, back_sem).start()

        @pl.when(turn_index > 0)
        def _():
            return_copy(group, my_member).start()

        return carry

    lax.fori_loop(0, GROUPS, work, 0)

    tile = 256

    def grad_copy(n, part):
        source, target = ((part_in, sums_in_ref), (part_out, sums_out_ref))[n]
        if part == 0:
            return pltpu.make_async_copy(source.at[0], target.at[0], g_recv_sem.at[n, 0])
        return pltpu.make_async_remote_copy(
            src_ref=source.at[part],
            dst_ref=target.at[parts - part],
            send_sem=g_send_sem.at[n, part],
            recv_sem=g_recv_sem.at[n, parts - part],
            device_id={"dp": (my_dp + part) % parts},
            device_id_type=MESH,
        )

    for part in list(range(1, parts)) + [0]:
        for n, (left, right, target) in enumerate(
            ((rows_x, d_pre, part_in), (rows_dy, scaled, part_out))
        ):

            def grads(t, carry, left=left, right=right, target=target, part=part):
                columns = pl.ds(pl.multiple_of(t * tile, tile), tile)
                target[part, columns] = contract_first(left[:, columns], right[part]).astype(BF)
                return carry

            lax.fori_loop(0, width // tile, grads, 0)
            grad_copy(n, part).start()

    d_left, d_right, g_0, g_1 = None, None, None, None
    for step in order:
        group = paired(my_group, step)
        to_x, to_dy, to_line_0, to_line_1 = selectors(group)
        await_group(back_buf, back_sem, group)
        back = back_buf[group]
        terms = (
            matmul(to_x, back),
            matmul(to_dy, back),
            matmul(to_line_0, back[:, :128]),
            matmul(to_line_1, back[:, :128]),
        )
        if d_left is None:
            d_left, d_right, g_0, g_1 = terms
        else:
            d_left, d_right, g_0, g_1 = (
                d_left + terms[0],
                d_right + terms[1],
                g_0 + terms[2],
                g_1 + terms[3],
            )
    d_tokens_ref[:, :half] = d_left.astype(BF)
    d_tokens_ref[:, half:] = d_right.astype(BF)
    first_gate = jnp.sum(jnp.where(at_slot_0, g_0, 0.0), axis=1, keepdims=True)
    second_gate = jnp.sum(jnp.where(at_slot_1, g_1, 0.0), axis=1, keepdims=True)
    gate_grad_ref[...] = jnp.where(lanes(tok_rows, 2) == 0, first_gate, second_gate).astype(BF)

    for step in range(GROUPS):
        group = paired(my_group, step)
        for turn in range(size):
            if step or turn:
                member = (my_member + turn) % size
                dispatch_copy(group, member).wait_send()
                return_copy(group, member).wait_send()
    for turn in range(1, parts):
        for n, source in enumerate((w_in_ref, w_out_ref)):
            block = source.at[0]
            pltpu.make_async_copy(block, block, w_send_sem.at[n, turn]).wait()
            grad_copy(n, turn).wait_send()
    for part in range(parts):
        for n, target in enumerate((sums_in_ref, sums_out_ref)):
            block = target.at[part]
            pltpu.make_async_copy(block, block, g_recv_sem.at[n, part]).wait()


def shards(experts, parts, tokens, out_grad, gates, expert_ids, w_in, w_out):
    tok_rows, width = tokens.shape
    hidden = w_in.shape[2]
    cap = 3 * tok_rows // experts
    chunk = -(-(2 * cap + 1) // 16) * 16
    span = experts // GROUPS * chunk
    slots = experts // GROUPS * cap
    vmem = pl.BlockSpec(memory_space=pltpu.VMEM)
    hbm = pl.BlockSpec(memory_space=pl.ANY)
    dma = pltpu.SemaphoreType.DMA
    d_tokens, gate_grad, sums_in, sums_out = pl.pallas_call(
        functools.partial(kernel, experts, parts, cap, chunk),
        out_shape=(
            jax.ShapeDtypeStruct((tok_rows, width), BF),
            jax.ShapeDtypeStruct((tok_rows, 2), BF),
            jax.ShapeDtypeStruct((parts, width, hidden), BF),
            jax.ShapeDtypeStruct((parts, width, hidden), BF),
        ),
        in_specs=[vmem, vmem, vmem, vmem, hbm, hbm],
        out_specs=(vmem, vmem, hbm, hbm),
        scratch_shapes=[
            pltpu.VMEM((GROUPS, span, width), BF),
            pltpu.VMEM((GROUPS, span, width), BF),
            pltpu.VMEM((GROUPS, span, width // 2), BF),
            pltpu.VMEM((GROUPS, span, width // 2), BF),
            pltpu.VMEM((slots, span), BF),
            pltpu.VMEM((slots, span), BF),
            pltpu.VMEM((slots, span), BF),
            pltpu.VMEM((parts, width, hidden), BF),
            pltpu.VMEM((parts, width, hidden), BF),
            pltpu.VMEM((GROUPS * slots, width), BF),
            pltpu.VMEM((GROUPS * slots, width), BF),
            pltpu.VMEM((parts, GROUPS * slots, hidden), BF),
            pltpu.VMEM((parts, GROUPS * slots, hidden), BF),
            pltpu.VMEM((parts, width, hidden), BF),
            pltpu.VMEM((parts, width, hidden), BF),
            dma((experts,)),
            dma((experts,)),
            dma((experts,)),
            dma((experts,)),
            dma((2, parts)),
            dma((2, parts)),
            dma((2, parts)),
            dma((2, parts)),
        ],
        compiler_params=pltpu.CompilerParams(
            collective_id=0, has_side_effects=True, vmem_limit_bytes=56 * 1024 * 1024
        ),
        cost_estimate=pl.CostEstimate(
            flops=10 * GROUPS * slots * width * width,
            bytes_accessed=16 * width * width,
            transcendentals=GROUPS * slots * width,
        ),
    )(tokens, out_grad, gates, expert_ids, w_in, w_out)
    return (
        d_tokens,
        gate_grad,
        jnp.sum(sums_in.astype(F32), axis=0)[None],
        jnp.sum(sums_out.astype(F32), axis=0)[None],
    )


def solution(mesh):
    split = P(("dp", "expert"), None)
    weights = P("expert", None, "dp")
    return jax.shard_map(
        functools.partial(shards, mesh.shape["expert"], mesh.shape["dp"]),
        mesh=mesh,
        in_specs=(split, split, split, split, weights, weights),
        out_specs=(split, split, weights, weights),
        check_vma=False,
    )
```

```python
import functools

import jax
import jax.numpy as jnp
from jax import lax
from jax.experimental import pallas as pl
from jax.experimental.pallas import tpu as pltpu
from jax.sharding import PartitionSpec as P

gelu_scale = 0.7978845608028654
cubic_coef = 0.044715
MESH = pl.DeviceIdType.MESH
GROUPS = 4
BF = jnp.bfloat16
F32 = jnp.float32


def paired(group, step):
    return 2 * ((group // 2 + step // 2) % 2) + (group % 2 + step % 2) % 2


def contract_first(a, b):
    return lax.dot_general(a, b, (((0,), (0,)), ((), ())), preferred_element_type=F32)


def contract_last(a, b):
    return lax.dot_general(a, b, (((1,), (1,)), ((), ())), preferred_element_type=F32)


def matmul(a, b):
    return jnp.dot(a, b, preferred_element_type=F32)


def lanes(rows, columns):
    return lax.broadcasted_iota(jnp.int32, (rows, columns), 1)


def ones_at(*conditions):
    hit = conditions[0]
    for other in conditions[1:]:
        hit = hit | other
    return jnp.where(hit, 1.0, 0.0).astype(BF)


def kernel(
    experts,
    parts,
    cap,
    chunk,
    tokens_ref,
    out_grad_ref,
    gates_ref,
    ids_ref,
    w_in_ref,
    w_out_ref,
    d_tokens_ref,
    gate_grad_ref,
    sums_in_ref,
    sums_out_ref,
    send_buf,
    recv_buf,
    ret_buf,
    back_buf,
    ret_gate,
    back_gate,
    picks,
    weights_in,
    weights_out,
    rows_x,
    rows_dy,
    d_pre,
    active,
    part_in,
    part_out,
    send_sem,
    recv_sem,
    ret_sem,
    back_sem,
    ret_gate_sem,
    back_gate_sem,
    w_send_sem,
    w_recv_sem,
    g_send_sem,
    g_recv_sem,
):
    size = experts // GROUPS
    span = size * chunk
    slots = size * cap
    line = 16
    tok_rows, width = tokens_ref.shape
    half, quarter = width // 2, width // 4
    me = lax.axis_index("expert")
    my_dp = lax.axis_index("dp")
    my_group, my_member = me // size, me % size

    def expert_device(group, member):
        return {"expert": group * size + member}

    barrier = pltpu.get_barrier_semaphore()
    for step in range(GROUPS):
        for turn in range(size):
            if step or turn:
                pl.semaphore_signal(
                    barrier,
                    inc=1,
                    device_id=expert_device(paired(my_group, step), (my_member + turn) % size),
                    device_id_type=MESH,
                )
    for turn in range(1, parts):
        pl.semaphore_signal(
            barrier, inc=1, device_id={"dp": (my_dp + turn) % parts}, device_id_type=MESH
        )

    own_w = [
        pltpu.make_async_copy(w_in_ref.at[0], weights_in.at[0], w_recv_sem.at[0, 0]),
        pltpu.make_async_copy(w_out_ref.at[0], weights_out.at[0], w_recv_sem.at[1, 0]),
    ]
    for copy in own_w:
        copy.start()

    same = lax.broadcasted_iota(jnp.int32, (tok_rows, tok_rows), 0) == lanes(tok_rows, tok_rows)

    def column(row):
        return jnp.sum(jnp.where(same, row, 0.0), axis=1, keepdims=True)

    def row(values):
        return jnp.sum(jnp.where(same, values, 0.0), axis=0, keepdims=True)

    ids, gates = ids_ref[...].astype(F32), gates_ref[...].astype(F32)
    id_0, id_1 = column(ids[0:1]).astype(jnp.int32), column(ids[1:2]).astype(jnp.int32)
    gate_0, gate_1 = column(gates[0:1]), column(gates[1:2])
    named = lanes(tok_rows, 128)
    named_0, named_1 = named == id_0, named == id_1
    later = lax.broadcasted_iota(jnp.int32, (tok_rows, tok_rows), 0) > lanes(tok_rows, tok_rows)
    earlier = matmul(ones_at(later), ones_at(named_0, named_1))
    slot_0 = jnp.sum(jnp.where(named_0, earlier, 0.0), axis=1, keepdims=True).astype(jnp.int32)
    slot_1 = jnp.sum(jnp.where(named_1, earlier, 0.0), axis=1, keepdims=True).astype(jnp.int32)
    place_0, place_1 = id_0 * chunk + slot_0, id_1 * chunk + slot_1
    line_0, line_1 = id_0 * line, id_1 * line

    def selector(group, block):
        lane = lanes(tok_rows, span) + (group * span - block * cap)
        return ones_at(lane == place_0, lane == place_1)

    def gated_selector(group, block):
        lane = lanes(tok_rows, span) + (group * span - block * cap)
        return jnp.where(
            lane == place_0, gate_0, jnp.where(lane == place_1, gate_1, 0.0)
        ).astype(BF)

    def chunk_rows(member):
        return pl.ds(pl.multiple_of(member * chunk, 16), chunk)

    def dispatch_copy(group, member):
        return pltpu.make_async_remote_copy(
            src_ref=send_buf.at[group, chunk_rows(member)],
            dst_ref=recv_buf.at[my_group, chunk_rows(my_member)],
            send_sem=send_sem.at[group * size + member],
            recv_sem=recv_sem.at[me],
            device_id=expert_device(group, member),
            device_id_type=MESH,
        )

    def return_copy(group, member):
        return pltpu.make_async_remote_copy(
            src_ref=ret_buf.at[group, chunk_rows(member)],
            dst_ref=back_buf.at[my_group, chunk_rows(my_member)],
            send_sem=ret_sem.at[group * size + member],
            recv_sem=back_sem.at[me],
            device_id=expert_device(group, member),
            device_id_type=MESH,
        )

    def line_rows(member):
        return pl.ds(pl.multiple_of(member * line, 16), line)

    def gate_copy(group, member):
        return pltpu.make_async_remote_copy(
            src_ref=ret_gate.at[group, line_rows(member)],
            dst_ref=back_gate.at[my_group, line_rows(my_member)],
            send_sem=ret_gate_sem.at[group * size + member],
            recv_sem=back_gate_sem.at[me],
            device_id=expert_device(group, member),
            device_id_type=MESH,
        )

    def local_copy(source, target, sems, rows):
        return pltpu.make_async_copy(
            source.at[my_group, rows], target.at[my_group, rows], sems.at[me]
        )

    def await_group(target, sems, group, rows):
        for member in range(size):
            block = target.at[group, pl.ds(member * rows, rows)]
            pltpu.make_async_copy(block, block, sems.at[group * size + member]).wait()

    def fill(group):
        packed = contract_first(selector(group, 0), tokens_ref[:, :half])
        packed += contract_first(selector(group, 1), tokens_ref[:, half:])
        packed += contract_first(gated_selector(group, 2), out_grad_ref[:, :half])
        packed += contract_first(gated_selector(group, 3), out_grad_ref[:, half:])
        send_buf[group] = packed.astype(BF)

    for step in (3, 2, 1, 0):
        group = paired(my_group, step)
        fill(group)
        if step == 3:
            pl.semaphore_wait(barrier, experts - 1 + parts - 1)
        for turn in range(size):
            member = (my_member + turn) % size
            if step or turn:
                dispatch_copy(group, member).start()
            else:
                local_copy(send_buf, recv_buf, recv_sem, chunk_rows(my_member)).start()
        if step == 3:
            for turn in range(1, parts):
                for n, (source, target) in enumerate(
                    ((w_in_ref, weights_in), (w_out_ref, weights_out))
                ):
                    pltpu.make_async_remote_copy(
                        src_ref=source.at[0],
                        dst_ref=target.at[parts - turn],
                        send_sem=w_send_sem.at[n, turn],
                        recv_sem=w_recv_sem.at[n, parts - turn],
                        device_id={"dp": (my_dp + turn) % parts},
                        device_id_type=MESH,
                    ).start()

    slot = lax.broadcasted_iota(jnp.int32, (slots, 1), 0)
    source = slot // cap
    within = slot - source * cap
    for block in range(4):
        picks[block] = ones_at(lanes(slots, span) == source * chunk + within + block * cap)
    to_line = ones_at(lanes(slots, size * line) == source * line)
    at_within = lanes(slots, 128) == within

    for copy in own_w:
        copy.wait()
    for part in range(1, parts):
        for n, target in enumerate((weights_in, weights_out)):
            block = target.at[part]
            pltpu.make_async_copy(block, block, w_recv_sem.at[n, part]).wait()

    order = (0, 1, 3, 2)

    def work(turn_index, carry):
        step = turn_index + (turn_index // 2) * (5 - 2 * turn_index)
        group = paired(my_group, step)
        await_group(recv_buf, recv_sem, group, chunk)
        rows = pl.ds(pl.multiple_of(turn_index * slots, 16), slots)
        got = recv_buf[group]
        rows_x[rows, :half] = matmul(picks[0], got).astype(BF)
        rows_x[rows, half:] = matmul(picks[1], got).astype(BF)
        rows_dy[rows, :half] = matmul(picks[2], got).astype(BF)
        rows_dy[rows, half:] = matmul(picks[3], got).astype(BF)
        x, dy = rows_x[rows], rows_dy[rows]
        dx = None
        gate_slot = None
        for part in range(parts):
            v = matmul(x, weights_in[part])
            dy_proj = matmul(dy, weights_out[part])
            tanh_inner = jnp.tanh(gelu_scale * (v + cubic_coef * v * v * v))
            activated = (0.5 * v * (1.0 + tanh_inner)).astype(BF)
            slope = 0.5 * (1.0 + tanh_inner) + 0.5 * v * (
                1.0 - tanh_inner * tanh_inner
            ) * gelu_scale * (1.0 + 3.0 * cubic_coef * v * v)
            d_pre_part = (dy_proj * slope).astype(BF)
            d_pre[part, rows] = d_pre_part
            active[part, rows] = activated
            gate_part = jnp.sum(activated.astype(F32) * dy_proj, axis=1, keepdims=True)
            dx_part = contract_last(d_pre_part, weights_in[part])
            dx = dx_part if dx is None else dx + dx_part
            gate_slot = gate_part if gate_slot is None else gate_slot + gate_part
        dx = dx.astype(BF)
        packed = contract_first(picks[0], dx[:, :quarter])
        for block in range(1, 4):
            packed += contract_first(
                picks[block], dx[:, block * quarter : (block + 1) * quarter]
            )
        ret_buf[group] = packed.astype(BF)
        ret_gate[group] = contract_first(
            to_line, jnp.where(at_within, gate_slot, 0.0).astype(BF)
        ).astype(BF)

        for turn in range(1, size):
            return_copy(group, (my_member + turn) % size).start()
            gate_copy(group, (my_member + turn) % size).start()

        @pl.when(turn_index == 0)
        def _():
            local_copy(ret_buf, back_buf, back_sem, chunk_rows(my_member)).start()
            local_copy(ret_gate, back_gate, back_gate_sem, line_rows(my_member)).start()

        @pl.when(turn_index > 0)
        def _():
            return_copy(group, my_member).start()
            gate_copy(group, my_member).start()

        return carry

    lax.fori_loop(0, GROUPS, work, 0)

    tile = 256

    def grad_copy(n, part):
        source, target = ((part_in, sums_in_ref), (part_out, sums_out_ref))[n]
        if part == 0:
            return pltpu.make_async_copy(source.at[0], target.at[0], g_recv_sem.at[n, 0])
        return pltpu.make_async_remote_copy(
            src_ref=source.at[part],
            dst_ref=target.at[parts - part],
            send_sem=g_send_sem.at[n, part],
            recv_sem=g_recv_sem.at[n, parts - part],
            device_id={"dp": (my_dp + part) % parts},
            device_id_type=MESH,
        )

    for part in list(range(1, parts)) + [0]:
        for n, (left, right, target) in enumerate(
            ((rows_x, d_pre, part_in), (rows_dy, active, part_out))
        ):

            def grads(t, carry, left=left, right=right, target=target, part=part):
                columns = pl.ds(pl.multiple_of(t * tile, tile), tile)
                target[part, columns] = contract_first(left[:, columns], right[part]).astype(BF)
                return carry

            lax.fori_loop(0, width // tile, grads, 0)
            grad_copy(n, part).start()

    totals = None
    for step in order:
        group = paired(my_group, step)
        selectors = [selector(group, block) for block in range(4)]
        lane = lanes(tok_rows, size * line) + group * size * line
        from_lines = ones_at(lane == line_0), ones_at(lane == line_1)
        await_group(back_gate, back_gate_sem, group, line)
        await_group(back_buf, back_sem, group, chunk)
        back, lines = back_buf[group], back_gate[group]
        terms = [matmul(chosen, back) for chosen in selectors]
        terms += [matmul(chosen, lines) for chosen in from_lines]
        totals = terms if totals is None else [a + b for a, b in zip(totals, terms)]
    for block in range(4):
        d_tokens_ref[:, block * quarter : (block + 1) * quarter] = totals[block].astype(BF)
    first_gate = jnp.sum(jnp.where(named == slot_0, totals[4], 0.0), axis=1, keepdims=True)
    second_gate = jnp.sum(jnp.where(named == slot_1, totals[5], 0.0), axis=1, keepdims=True)
    gate_grad_ref[0:1] = row(first_gate / gate_0).astype(BF)
    gate_grad_ref[1:2] = row(second_gate / gate_1).astype(BF)

    for step in range(GROUPS):
        group = paired(my_group, step)
        for turn in range(size):
            if step or turn:
                member = (my_member + turn) % size
                dispatch_copy(group, member).wait_send()
                return_copy(group, member).wait_send()
                gate_copy(group, member).wait_send()
    for turn in range(1, parts):
        for n, source in enumerate((w_in_ref, w_out_ref)):
            block = source.at[0]
            pltpu.make_async_copy(block, block, w_send_sem.at[n, turn]).wait()
            grad_copy(n, turn).wait_send()
    for part in range(parts):
        for n, target in enumerate((sums_in_ref, sums_out_ref)):
            block = target.at[part]
            pltpu.make_async_copy(block, block, g_recv_sem.at[n, part]).wait()


def shards(experts, parts, tokens, out_grad, gates, expert_ids, w_in, w_out):
    tok_rows, width = tokens.shape
    hidden = w_in.shape[2]
    cap = 3 * tok_rows // experts
    chunk = -(-4 * cap // 16) * 16
    span = experts // GROUPS * chunk
    slots = experts // GROUPS * cap
    vmem = pl.BlockSpec(memory_space=pltpu.VMEM)
    hbm = pl.BlockSpec(memory_space=pltpu.HBM)
    free = pl.BlockSpec(memory_space=pl.ANY)
    dma = pltpu.SemaphoreType.DMA
    d_tokens, gate_grad, sums_in, sums_out = pl.pallas_call(
        functools.partial(kernel, experts, parts, cap, chunk),
        out_shape=(
            jax.ShapeDtypeStruct((tok_rows, width), BF),
            jax.ShapeDtypeStruct((2, tok_rows), BF),
            jax.ShapeDtypeStruct((parts, width, hidden), BF),
            jax.ShapeDtypeStruct((parts, width, hidden), BF),
        ),
        in_specs=[vmem, vmem, vmem, vmem, hbm, hbm],
        out_specs=(vmem, vmem, free, free),
        scratch_shapes=[
            pltpu.VMEM((GROUPS, span, width // 2), BF),
            pltpu.VMEM((GROUPS, span, width // 2), BF),
            pltpu.VMEM((GROUPS, span, width // 4), BF),
            pltpu.VMEM((GROUPS, span, width // 4), BF),
            pltpu.VMEM((GROUPS, experts // GROUPS * 16, 128), BF),
            pltpu.VMEM((GROUPS, experts // GROUPS * 16, 128), BF),
            pltpu.VMEM((4, slots, span), BF),
            pltpu.VMEM((parts, width, hidden), BF),
            pltpu.VMEM((parts, width, hidden), BF),
            pltpu.VMEM((GROUPS * slots, width), BF),
            pltpu.VMEM((GROUPS * slots, width), BF),
            pltpu.VMEM((parts, GROUPS * slots, hidden), BF),
            pltpu.VMEM((parts, GROUPS * slots, hidden), BF),
            pltpu.VMEM((parts, width, hidden), BF),
            pltpu.VMEM((parts, width, hidden), BF),
            dma((experts,)),
            dma((experts,)),
            dma((experts,)),
            dma((experts,)),
            dma((experts,)),
            dma((experts,)),
            dma((2, parts)),
            dma((2, parts)),
            dma((2, parts)),
            dma((2, parts)),
        ],
        compiler_params=pltpu.CompilerParams(
            collective_id=0, has_side_effects=True, vmem_limit_bytes=36 * 1024 * 1024
        ),
        cost_estimate=pl.CostEstimate(
            flops=10 * GROUPS * slots * width * width,
            bytes_accessed=16 * width * width,
            transcendentals=GROUPS * slots * width,
        ),
    )(tokens, out_grad, gates.T, expert_ids.T, w_in, w_out)
    return (
        d_tokens,
        gate_grad.T,
        jnp.sum(sums_in.astype(F32), axis=0)[None],
        jnp.sum(sums_out.astype(F32), axis=0)[None],
    )


def solution(mesh):
    split = P(("dp", "expert"), None)
    weights = P("expert", None, "dp")
    return jax.shard_map(
        functools.partial(shards, mesh.shape["expert"], mesh.shape["dp"]),
        mesh=mesh,
        in_specs=(split, split, split, split, weights, weights),
        out_specs=(split, split, weights, weights),
        check_vma=False,
    )
```

```python
import functools

import jax
import jax.numpy as jnp
from jax import lax
from jax.experimental import pallas as pl
from jax.experimental.pallas import tpu as pltpu
from jax.sharding import PartitionSpec as P

gelu_scale = 0.7978845608028654
cubic_coef = 0.044715
MESH = pl.DeviceIdType.MESH
GROUPS = 4
BF = jnp.bfloat16
F32 = jnp.float32


def paired(group, step):
    return 2 * ((group // 2 + step // 2) % 2) + (group % 2 + step % 2) % 2


def contract_first(a, b):
    return lax.dot_general(a, b, (((0,), (0,)), ((), ())), preferred_element_type=F32)


def contract_last(a, b):
    return lax.dot_general(a, b, (((1,), (1,)), ((), ())), preferred_element_type=F32)


def matmul(a, b):
    return jnp.dot(a, b, preferred_element_type=F32)


def lanes(rows, columns):
    return lax.broadcasted_iota(jnp.int32, (rows, columns), 1)


def ones_at(*conditions):
    hit = conditions[0]
    for other in conditions[1:]:
        hit = hit | other
    return jnp.where(hit, 1.0, 0.0).astype(BF)


def kernel(
    experts,
    parts,
    cap,
    chunk,
    tokens_hbm,
    out_grad_hbm,
    gates_ref,
    ids_ref,
    w_in_ref,
    w_out_ref,
    d_tokens_ref,
    gate_grad_ref,
    sums_in_ref,
    sums_out_ref,
    tokens_ref,
    out_grad_ref,
    send_buf,
    recv_buf,
    ret_buf,
    back_buf,
    ret_gate,
    back_gate,
    picks,
    weights_in,
    weights_out,
    rows_x,
    rows_dy,
    d_pre,
    active,
    part_in,
    part_out,
    send_sem,
    recv_sem,
    ret_sem,
    back_sem,
    ret_gate_sem,
    back_gate_sem,
    w_send_sem,
    w_recv_sem,
    g_send_sem,
    g_recv_sem,
    token_sem,
):
    size = experts // GROUPS
    span = size * chunk
    slots = size * cap
    line = 16
    tok_rows, width = tokens_ref.shape
    half, quarter = width // 2, width // 4
    me = lax.axis_index("expert")
    my_dp = lax.axis_index("dp")
    my_group, my_member = me // size, me % size

    def expert_device(group, member):
        return {"expert": group * size + member}

    own_rows = [
        pltpu.make_async_copy(tokens_hbm, tokens_ref, token_sem.at[0]),
        pltpu.make_async_copy(out_grad_hbm, out_grad_ref, token_sem.at[1]),
    ]
    for copy in own_rows:
        copy.start()

    barrier = pltpu.get_barrier_semaphore()
    for step in range(GROUPS):
        for turn in range(size):
            if step or turn:
                pl.semaphore_signal(
                    barrier,
                    inc=1,
                    device_id=expert_device(paired(my_group, step), (my_member + turn) % size),
                    device_id_type=MESH,
                )
    for turn in range(1, parts):
        pl.semaphore_signal(
            barrier, inc=1, device_id={"dp": (my_dp + turn) % parts}, device_id_type=MESH
        )

    own_w = [
        pltpu.make_async_copy(w_in_ref.at[0], weights_in.at[0], w_recv_sem.at[0, 0]),
        pltpu.make_async_copy(w_out_ref.at[0], weights_out.at[0], w_recv_sem.at[1, 0]),
    ]
    for copy in own_w:
        copy.start()

    same = lax.broadcasted_iota(jnp.int32, (tok_rows, tok_rows), 0) == lanes(tok_rows, tok_rows)

    def column(row):
        return jnp.sum(jnp.where(same, row, 0.0), axis=1, keepdims=True)

    def row(values):
        return jnp.sum(jnp.where(same, values, 0.0), axis=0, keepdims=True)

    ids, gates = ids_ref[...].astype(F32), gates_ref[...].astype(F32)
    id_0, id_1 = column(ids[0:1]).astype(jnp.int32), column(ids[1:2]).astype(jnp.int32)
    gate_0, gate_1 = column(gates[0:1]), column(gates[1:2])
    named = lanes(tok_rows, 128)
    named_0, named_1 = named == id_0, named == id_1
    later = lax.broadcasted_iota(jnp.int32, (tok_rows, tok_rows), 0) > lanes(tok_rows, tok_rows)
    earlier = matmul(ones_at(later), ones_at(named_0, named_1))
    slot_0 = jnp.sum(jnp.where(named_0, earlier, 0.0), axis=1, keepdims=True).astype(jnp.int32)
    slot_1 = jnp.sum(jnp.where(named_1, earlier, 0.0), axis=1, keepdims=True).astype(jnp.int32)
    place_0, place_1 = id_0 * chunk + slot_0, id_1 * chunk + slot_1
    line_0, line_1 = id_0 * line, id_1 * line

    def selector(group, block):
        lane = lanes(tok_rows, span) + (group * span - block * cap)
        return ones_at(lane == place_0, lane == place_1)

    def chunk_selector(start, block):
        lane = lanes(tok_rows, chunk) + (start - block * cap)
        return ones_at(lane == place_0, lane == place_1)

    def gated_selector(start, block):
        lane = lanes(tok_rows, chunk) + (start - block * cap)
        return jnp.where(
            lane == place_0, gate_0, jnp.where(lane == place_1, gate_1, 0.0)
        ).astype(BF)

    def chunk_rows(member):
        return pl.ds(pl.multiple_of(member * chunk, 16), chunk)

    def dispatch_copy(group, member):
        return pltpu.make_async_remote_copy(
            src_ref=send_buf.at[group, chunk_rows(member)],
            dst_ref=recv_buf.at[my_group, chunk_rows(my_member)],
            send_sem=send_sem.at[group * size + member],
            recv_sem=recv_sem.at[me],
            device_id=expert_device(group, member),
            device_id_type=MESH,
        )

    def return_copy(group, member):
        return pltpu.make_async_remote_copy(
            src_ref=ret_buf.at[group, chunk_rows(member)],
            dst_ref=back_buf.at[my_group, chunk_rows(my_member)],
            send_sem=ret_sem.at[group * size + member],
            recv_sem=back_sem.at[me],
            device_id=expert_device(group, member),
            device_id_type=MESH,
        )

    def line_rows(member):
        return pl.ds(pl.multiple_of(member * line, 16), line)

    def gate_copy(group, member):
        return pltpu.make_async_remote_copy(
            src_ref=ret_gate.at[group, line_rows(member)],
            dst_ref=back_gate.at[my_group, line_rows(my_member)],
            send_sem=ret_gate_sem.at[group * size + member],
            recv_sem=back_gate_sem.at[me],
            device_id=expert_device(group, member),
            device_id_type=MESH,
        )

    def local_copy(source, target, sems, rows):
        return pltpu.make_async_copy(
            source.at[my_group, rows], target.at[my_group, rows], sems.at[me]
        )

    def await_group(target, sems, group, rows):
        for member in range(size):
            block = target.at[group, pl.ds(member * rows, rows)]
            pltpu.make_async_copy(block, block, sems.at[group * size + member]).wait()

    def fill(group, member):
        start = (group * size + member) * chunk
        packed = contract_first(chunk_selector(start, 0), tokens_ref[:, :half])
        packed += contract_first(chunk_selector(start, 1), tokens_ref[:, half:])
        packed += contract_first(gated_selector(start, 2), out_grad_ref[:, :half])
        packed += contract_first(gated_selector(start, 3), out_grad_ref[:, half:])
        send_buf[group, chunk_rows(member)] = packed.astype(BF)

    def fill_and_send(step, turn):
        group, member = paired(my_group, step), (my_member + turn) % size
        fill(group, member)
        dispatch_copy(group, member).start()

    for copy in own_rows:
        copy.wait()
    fill(paired(my_group, 3), my_member)
    pl.semaphore_wait(barrier, experts - 1 + parts - 1)
    dispatch_copy(paired(my_group, 3), my_member).start()
    for turn in range(1, parts):
        for n, (source, target) in enumerate(((w_in_ref, weights_in), (w_out_ref, weights_out))):
            pltpu.make_async_remote_copy(
                src_ref=source.at[0],
                dst_ref=target.at[parts - turn],
                send_sem=w_send_sem.at[n, turn],
                recv_sem=w_recv_sem.at[n, parts - turn],
                device_id={"dp": (my_dp + turn) % parts},
                device_id_type=MESH,
            ).start()

    def others(count, carry):
        fill_and_send(3 - count // size, count % size)
        return carry

    lax.fori_loop(1, 3 * size, others, 0)
    fill(my_group, my_member)
    local_copy(send_buf, recv_buf, recv_sem, chunk_rows(my_member)).start()
    lax.fori_loop(3 * size + 1, 4 * size, others, 0)

    slot = lax.broadcasted_iota(jnp.int32, (slots, 1), 0)
    source = slot // cap
    within = slot - source * cap
    for block in range(4):
        picks[block] = ones_at(lanes(slots, span) == source * chunk + within + block * cap)
    to_line = ones_at(lanes(slots, size * line) == source * line)
    at_within = lanes(slots, 128) == within

    for copy in own_w:
        copy.wait()
    for part in range(1, parts):
        for n, target in enumerate((weights_in, weights_out)):
            block = target.at[part]
            pltpu.make_async_copy(block, block, w_recv_sem.at[n, part]).wait()

    order = (0, 1, 3, 2)

    def work(turn_index, carry):
        step = turn_index + (turn_index // 2) * (5 - 2 * turn_index)
        group = paired(my_group, step)
        await_group(recv_buf, recv_sem, group, chunk)
        rows = pl.ds(pl.multiple_of(turn_index * slots, 16), slots)
        got = recv_buf[group]
        rows_x[rows, :half] = matmul(picks[0], got).astype(BF)
        rows_x[rows, half:] = matmul(picks[1], got).astype(BF)
        rows_dy[rows, :half] = matmul(picks[2], got).astype(BF)
        rows_dy[rows, half:] = matmul(picks[3], got).astype(BF)
        x, dy = rows_x[rows], rows_dy[rows]
        dx = None
        gate_slot = None
        for part in range(parts):
            v = matmul(x, weights_in[part])
            dy_proj = matmul(dy, weights_out[part])
            tanh_inner = jnp.tanh(gelu_scale * (v + cubic_coef * v * v * v))
            activated = (0.5 * v * (1.0 + tanh_inner)).astype(BF)
            slope = 0.5 * (1.0 + tanh_inner) + 0.5 * v * (
                1.0 - tanh_inner * tanh_inner
            ) * gelu_scale * (1.0 + 3.0 * cubic_coef * v * v)
            d_pre_part = (dy_proj * slope).astype(BF)
            d_pre[part, rows] = d_pre_part
            active[part, rows] = activated
            gate_part = jnp.sum(activated.astype(F32) * dy_proj, axis=1, keepdims=True)
            dx_part = contract_last(d_pre_part, weights_in[part])
            dx = dx_part if dx is None else dx + dx_part
            gate_slot = gate_part if gate_slot is None else gate_slot + gate_part
        dx = dx.astype(BF)
        packed = contract_first(picks[0], dx[:, :quarter])
        for block in range(1, 4):
            packed += contract_first(
                picks[block], dx[:, block * quarter : (block + 1) * quarter]
            )
        ret_buf[group] = packed.astype(BF)
        ret_gate[group] = contract_first(
            to_line, jnp.where(at_within, gate_slot, 0.0).astype(BF)
        ).astype(BF)

        for turn in range(1, size):
            return_copy(group, (my_member + turn) % size).start()
            gate_copy(group, (my_member + turn) % size).start()

        @pl.when(turn_index == 0)
        def _():
            local_copy(ret_buf, back_buf, back_sem, chunk_rows(my_member)).start()
            local_copy(ret_gate, back_gate, back_gate_sem, line_rows(my_member)).start()

        @pl.when(turn_index > 0)
        def _():
            return_copy(group, my_member).start()
            gate_copy(group, my_member).start()

        return carry

    lax.fori_loop(0, GROUPS, work, 0)

    tile = 256

    def grad_copy(n, part):
        source, target = ((part_in, sums_in_ref), (part_out, sums_out_ref))[n]
        if part == 0:
            return pltpu.make_async_copy(source.at[0], target.at[0], g_recv_sem.at[n, 0])
        return pltpu.make_async_remote_copy(
            src_ref=source.at[part],
            dst_ref=target.at[parts - part],
            send_sem=g_send_sem.at[n, part],
            recv_sem=g_recv_sem.at[n, parts - part],
            device_id={"dp": (my_dp + part) % parts},
            device_id_type=MESH,
        )

    for part in list(range(1, parts)) + [0]:
        for n, (left, right, target) in enumerate(
            ((rows_x, d_pre, part_in), (rows_dy, active, part_out))
        ):

            def grads(t, carry, left=left, right=right, target=target, part=part):
                columns = pl.ds(pl.multiple_of(t * tile, tile), tile)
                target[part, columns] = contract_first(left[:, columns], right[part]).astype(BF)
                return carry

            lax.fori_loop(0, width // tile, grads, 0)
            grad_copy(n, part).start()

    totals = None
    for step in order:
        group = paired(my_group, step)
        selectors = [selector(group, block) for block in range(4)]
        lane = lanes(tok_rows, size * line) + group * size * line
        from_lines = ones_at(lane == line_0), ones_at(lane == line_1)
        await_group(back_gate, back_gate_sem, group, line)
        await_group(back_buf, back_sem, group, chunk)
        back, lines = back_buf[group], back_gate[group]
        terms = [matmul(chosen, back) for chosen in selectors]
        terms += [matmul(chosen, lines) for chosen in from_lines]
        totals = terms if totals is None else [a + b for a, b in zip(totals, terms)]
    for block in range(4):
        d_tokens_ref[:, block * quarter : (block + 1) * quarter] = totals[block].astype(BF)
    first_gate = jnp.sum(jnp.where(named == slot_0, totals[4], 0.0), axis=1, keepdims=True)
    second_gate = jnp.sum(jnp.where(named == slot_1, totals[5], 0.0), axis=1, keepdims=True)
    gate_grad_ref[0:1] = row(first_gate / gate_0).astype(BF)
    gate_grad_ref[1:2] = row(second_gate / gate_1).astype(BF)

    for step in range(GROUPS):
        group = paired(my_group, step)
        for turn in range(size):
            if step or turn:
                member = (my_member + turn) % size
                dispatch_copy(group, member).wait_send()
                return_copy(group, member).wait_send()
                gate_copy(group, member).wait_send()
    for turn in range(1, parts):
        for n, source in enumerate((w_in_ref, w_out_ref)):
            block = source.at[0]
            pltpu.make_async_copy(block, block, w_send_sem.at[n, turn]).wait()
            grad_copy(n, turn).wait_send()
    for part in range(parts):
        for n, target in enumerate((sums_in_ref, sums_out_ref)):
            block = target.at[part]
            pltpu.make_async_copy(block, block, g_recv_sem.at[n, part]).wait()


def stay(array):
    return pltpu.with_memory_space_constraint(array, pltpu.HBM)


def shards(experts, parts, tokens, out_grad, gates, expert_ids, w_in, w_out):
    tok_rows, width = tokens.shape
    hidden = w_in.shape[2]
    cap = 3 * tok_rows // experts
    chunk = -(-4 * cap // 16) * 16
    span = experts // GROUPS * chunk
    slots = experts // GROUPS * cap
    vmem = pl.BlockSpec(memory_space=pltpu.VMEM)
    hbm = pl.BlockSpec(memory_space=pltpu.HBM)
    free = pl.BlockSpec(memory_space=pl.ANY)
    dma = pltpu.SemaphoreType.DMA
    d_tokens, gate_grad, sums_in, sums_out = pl.pallas_call(
        functools.partial(kernel, experts, parts, cap, chunk),
        out_shape=(
            jax.ShapeDtypeStruct((tok_rows, width), BF),
            jax.ShapeDtypeStruct((2, tok_rows), BF),
            jax.ShapeDtypeStruct((parts, width, hidden), BF),
            jax.ShapeDtypeStruct((parts, width, hidden), BF),
        ),
        in_specs=[hbm, hbm, vmem, vmem, hbm, hbm],
        out_specs=(vmem, vmem, free, free),
        scratch_shapes=[
            pltpu.VMEM((tok_rows, width), BF),
            pltpu.VMEM((tok_rows, width), BF),
            pltpu.VMEM((GROUPS, span, width // 2), BF),
            pltpu.VMEM((GROUPS, span, width // 2), BF),
            pltpu.VMEM((GROUPS, span, width // 4), BF),
            pltpu.VMEM((GROUPS, span, width // 4), BF),
            pltpu.VMEM((GROUPS, experts // GROUPS * 16, 128), BF),
            pltpu.VMEM((GROUPS, experts // GROUPS * 16, 128), BF),
            pltpu.VMEM((4, slots, span), BF),
            pltpu.VMEM((parts, width, hidden), BF),
            pltpu.VMEM((parts, width, hidden), BF),
            pltpu.VMEM((GROUPS * slots, width), BF),
            pltpu.VMEM((GROUPS * slots, width), BF),
            pltpu.VMEM((parts, GROUPS * slots, hidden), BF),
            pltpu.VMEM((parts, GROUPS * slots, hidden), BF),
            pltpu.VMEM((parts, width, hidden), BF),
            pltpu.VMEM((parts, width, hidden), BF),
            dma((experts,)),
            dma((experts,)),
            dma((experts,)),
            dma((experts,)),
            dma((experts,)),
            dma((experts,)),
            dma((2, parts)),
            dma((2, parts)),
            dma((2, parts)),
            dma((2, parts)),
            dma((2,)),
        ],
        compiler_params=pltpu.CompilerParams(
            collective_id=0, has_side_effects=True, vmem_limit_bytes=36 * 1024 * 1024
        ),
        cost_estimate=pl.CostEstimate(
            flops=10 * GROUPS * slots * width * width,
            bytes_accessed=16 * width * width,
            transcendentals=GROUPS * slots * width,
        ),
    )(
        *map(stay, (tokens, out_grad, gates.T, expert_ids.T, w_in, w_out))
    )
    return (
        d_tokens,
        gate_grad.T,
        jnp.sum(sums_in.astype(F32), axis=0)[None],
        jnp.sum(sums_out.astype(F32), axis=0)[None],
    )


def solution(mesh):
    split = P(("dp", "expert"), None)
    weights = P("expert", None, "dp")
    return jax.shard_map(
        functools.partial(shards, mesh.shape["expert"], mesh.shape["dp"]),
        mesh=mesh,
        in_specs=(split, split, split, split, weights, weights),
        out_specs=(split, split, weights, weights),
        check_vma=False,
    )
```

```python
import functools

import jax
import jax.numpy as jnp
from jax import lax
from jax.experimental import pallas as pl
from jax.experimental.pallas import tpu as pltpu
from jax.sharding import PartitionSpec as P

gelu_scale = 0.7978845608028654
cubic_coef = 0.044715
MESH = pl.DeviceIdType.MESH
GROUPS = 4
BF = jnp.bfloat16
F32 = jnp.float32


def paired(group, step):
    return 2 * ((group // 2 + step // 2) % 2) + (group % 2 + step % 2) % 2


def contract_first(a, b):
    return lax.dot_general(a, b, (((0,), (0,)), ((), ())), preferred_element_type=F32)


def contract_last(a, b):
    return lax.dot_general(a, b, (((1,), (1,)), ((), ())), preferred_element_type=F32)


def matmul(a, b):
    return jnp.dot(a, b, preferred_element_type=F32)


def lanes(rows, columns):
    return lax.broadcasted_iota(jnp.int32, (rows, columns), 1)


def ones_at(*conditions):
    hit = conditions[0]
    for other in conditions[1:]:
        hit = hit | other
    return jnp.where(hit, 1.0, 0.0).astype(BF)


def kernel(
    experts,
    parts,
    cap,
    chunk,
    tokens_hbm,
    out_grad_hbm,
    gates_ref,
    ids_ref,
    w_in_ref,
    w_out_ref,
    d_tokens_ref,
    gate_grad_ref,
    sums_in_ref,
    sums_out_ref,
    quarters,
    send_buf,
    recv_buf,
    ret_buf,
    back_buf,
    ret_gate,
    back_gate,
    picks,
    weights_in,
    weights_out,
    rows_x,
    rows_dy,
    d_pre,
    active,
    part_in,
    part_out,
    send_sem,
    recv_sem,
    ret_sem,
    back_sem,
    ret_gate_sem,
    back_gate_sem,
    w_send_sem,
    w_recv_sem,
    g_send_sem,
    g_recv_sem,
    token_sem,
):
    size = experts // GROUPS
    span = size * chunk
    slots = size * cap
    line = 16
    tok_rows, width = tokens_hbm.shape
    half, quarter = width // 2, width // 4
    me = lax.axis_index("expert")
    my_dp = lax.axis_index("dp")
    my_group, my_member = me // size, me % size

    def expert_device(group, member):
        return {"expert": group * size + member}

    own_rows = [
        pltpu.make_async_copy(
            whole.at[:, pl.ds(side * half, half)],
            quarters.at[pl.ds((2 * n + side) * tok_rows, tok_rows)],
            token_sem.at[2 * n + side],
        )
        for n, whole in enumerate((tokens_hbm, out_grad_hbm))
        for side in range(2)
    ]
    for copy in own_rows:
        copy.start()

    barrier = pltpu.get_barrier_semaphore()
    for step in range(GROUPS):
        for turn in range(size):
            if step or turn:
                pl.semaphore_signal(
                    barrier,
                    inc=1,
                    device_id=expert_device(paired(my_group, step), (my_member + turn) % size),
                    device_id_type=MESH,
                )
    for turn in range(1, parts):
        pl.semaphore_signal(
            barrier, inc=1, device_id={"dp": (my_dp + turn) % parts}, device_id_type=MESH
        )

    own_w = [
        pltpu.make_async_copy(w_in_ref.at[0], weights_in.at[0], w_recv_sem.at[0, 0]),
        pltpu.make_async_copy(w_out_ref.at[0], weights_out.at[0], w_recv_sem.at[1, 0]),
    ]
    for copy in own_w:
        copy.start()

    same = lax.broadcasted_iota(jnp.int32, (tok_rows, tok_rows), 0) == lanes(tok_rows, tok_rows)

    def column(row):
        return jnp.sum(jnp.where(same, row, 0.0), axis=1, keepdims=True)

    def row(values):
        return jnp.sum(jnp.where(same, values, 0.0), axis=0, keepdims=True)

    ids, gates = ids_ref[...].astype(F32), gates_ref[...].astype(F32)
    id_0, id_1 = column(ids[0:1]).astype(jnp.int32), column(ids[1:2]).astype(jnp.int32)
    gate_0, gate_1 = column(gates[0:1]), column(gates[1:2])
    named = lanes(tok_rows, 128)
    named_0, named_1 = named == id_0, named == id_1
    later = lax.broadcasted_iota(jnp.int32, (tok_rows, tok_rows), 0) > lanes(tok_rows, tok_rows)
    earlier = matmul(ones_at(later), ones_at(named_0, named_1))
    slot_0 = jnp.sum(jnp.where(named_0, earlier, 0.0), axis=1, keepdims=True).astype(jnp.int32)
    slot_1 = jnp.sum(jnp.where(named_1, earlier, 0.0), axis=1, keepdims=True).astype(jnp.int32)
    place_0, place_1 = id_0 * chunk + slot_0, id_1 * chunk + slot_1
    line_0, line_1 = id_0 * line, id_1 * line

    def selector(group, block):
        lane = lanes(tok_rows, span) + (group * span - block * cap)
        return ones_at(lane == place_0, lane == place_1)

    def chunk_selector(start, block):
        lane = lanes(tok_rows, chunk) + (start - block * cap)
        return ones_at(lane == place_0, lane == place_1)

    def gated_selector(start, block):
        lane = lanes(tok_rows, chunk) + (start - block * cap)
        return jnp.where(
            lane == place_0, gate_0, jnp.where(lane == place_1, gate_1, 0.0)
        ).astype(BF)

    def chunk_rows(member):
        return pl.ds(pl.multiple_of(member * chunk, 16), chunk)

    def dispatch_copy(group, member):
        return pltpu.make_async_remote_copy(
            src_ref=send_buf.at[group, chunk_rows(member)],
            dst_ref=recv_buf.at[my_group, chunk_rows(my_member)],
            send_sem=send_sem.at[group * size + member],
            recv_sem=recv_sem.at[me],
            device_id=expert_device(group, member),
            device_id_type=MESH,
        )

    def return_copy(group, member):
        return pltpu.make_async_remote_copy(
            src_ref=ret_buf.at[group, chunk_rows(member)],
            dst_ref=back_buf.at[my_group, chunk_rows(my_member)],
            send_sem=ret_sem.at[group * size + member],
            recv_sem=back_sem.at[me],
            device_id=expert_device(group, member),
            device_id_type=MESH,
        )

    def line_rows(member):
        return pl.ds(pl.multiple_of(member * line, 16), line)

    def gate_copy(group, member):
        return pltpu.make_async_remote_copy(
            src_ref=ret_gate.at[group, line_rows(member)],
            dst_ref=back_gate.at[my_group, line_rows(my_member)],
            send_sem=ret_gate_sem.at[group * size + member],
            recv_sem=back_gate_sem.at[me],
            device_id=expert_device(group, member),
            device_id_type=MESH,
        )

    def local_copy(source, target, sems, rows):
        return pltpu.make_async_copy(
            source.at[my_group, rows], target.at[my_group, rows], sems.at[me]
        )

    def await_group(target, sems, group, rows):
        for member in range(size):
            block = target.at[group, pl.ds(member * rows, rows)]
            pltpu.make_async_copy(block, block, sems.at[group * size + member]).wait()

    def fill(group, member):
        start = (group * size + member) * chunk
        chosen = [chunk_selector(start, block) for block in (0, 1)]
        chosen += [gated_selector(start, block) for block in (2, 3)]
        packed = contract_first(jnp.concatenate(chosen, axis=0), quarters[...])
        send_buf[group, chunk_rows(member)] = packed.astype(BF)

    def fill_and_send(step, turn):
        group, member = paired(my_group, step), (my_member + turn) % size
        fill(group, member)
        dispatch_copy(group, member).start()

    for copy in own_rows:
        copy.wait()
    fill(paired(my_group, 3), my_member)
    pl.semaphore_wait(barrier, experts - 1 + parts - 1)
    dispatch_copy(paired(my_group, 3), my_member).start()
    for turn in range(1, parts):
        for n, (source, target) in enumerate(((w_in_ref, weights_in), (w_out_ref, weights_out))):
            pltpu.make_async_remote_copy(
                src_ref=source.at[0],
                dst_ref=target.at[parts - turn],
                send_sem=w_send_sem.at[n, turn],
                recv_sem=w_recv_sem.at[n, parts - turn],
                device_id={"dp": (my_dp + turn) % parts},
                device_id_type=MESH,
            ).start()

    def others(count, carry):
        fill_and_send(3 - count // size, count % size)
        return carry

    lax.fori_loop(1, 3 * size, others, 0)
    fill(my_group, my_member)
    local_copy(send_buf, recv_buf, recv_sem, chunk_rows(my_member)).start()
    lax.fori_loop(3 * size + 1, 4 * size, others, 0)

    slot = lax.broadcasted_iota(jnp.int32, (slots, 1), 0)
    source = slot // cap
    within = slot - source * cap
    for block in range(4):
        picks[block * slots : (block + 1) * slots] = ones_at(
            lanes(slots, span) == source * chunk + within + block * cap
        )
    to_line = ones_at(lanes(slots, size * line) == source * line)
    at_within = lanes(slots, 128) == within

    for copy in own_w:
        copy.wait()
    for part in range(1, parts):
        for n, target in enumerate((weights_in, weights_out)):
            block = target.at[part]
            pltpu.make_async_copy(block, block, w_recv_sem.at[n, part]).wait()

    order = (0, 1, 3, 2)

    def work(turn_index, carry):
        step = turn_index + (turn_index // 2) * (5 - 2 * turn_index)
        group = paired(my_group, step)
        await_group(recv_buf, recv_sem, group, chunk)
        rows = pl.ds(pl.multiple_of(turn_index * slots, 16), slots)
        got = recv_buf[group]
        got = matmul(picks[...], got).astype(BF)
        rows_x[rows, :half] = got[:slots]
        rows_x[rows, half:] = got[slots : 2 * slots]
        rows_dy[rows, :half] = got[2 * slots : 3 * slots]
        rows_dy[rows, half:] = got[3 * slots :]
        x, dy = rows_x[rows], rows_dy[rows]
        dx = None
        gate_slot = None
        for part in range(parts):
            v = matmul(x, weights_in[part])
            dy_proj = matmul(dy, weights_out[part])
            tanh_inner = jnp.tanh(gelu_scale * (v + cubic_coef * v * v * v))
            activated = (0.5 * v * (1.0 + tanh_inner)).astype(BF)
            slope = 0.5 * (1.0 + tanh_inner) + 0.5 * v * (
                1.0 - tanh_inner * tanh_inner
            ) * gelu_scale * (1.0 + 3.0 * cubic_coef * v * v)
            d_pre_part = (dy_proj * slope).astype(BF)
            d_pre[part, rows] = d_pre_part
            active[part, rows] = activated
            gate_part = jnp.sum(activated.astype(F32) * dy_proj, axis=1, keepdims=True)
            dx_part = contract_last(d_pre_part, weights_in[part])
            dx = dx_part if dx is None else dx + dx_part
            gate_slot = gate_part if gate_slot is None else gate_slot + gate_part
        dx = dx.astype(BF)
        stacked = [dx[:, block * quarter : (block + 1) * quarter] for block in range(4)]
        packed = contract_first(picks[...], jnp.concatenate(stacked, axis=0))
        ret_buf[group] = packed.astype(BF)
        ret_gate[group] = contract_first(
            to_line, jnp.where(at_within, gate_slot, 0.0).astype(BF)
        ).astype(BF)

        for turn in range(1, size):
            return_copy(group, (my_member + turn) % size).start()
            gate_copy(group, (my_member + turn) % size).start()

        @pl.when(turn_index == 0)
        def _():
            local_copy(ret_buf, back_buf, back_sem, chunk_rows(my_member)).start()
            local_copy(ret_gate, back_gate, back_gate_sem, line_rows(my_member)).start()

        @pl.when(turn_index > 0)
        def _():
            return_copy(group, my_member).start()
            gate_copy(group, my_member).start()

        return carry

    lax.fori_loop(0, GROUPS, work, 0)

    tile = 256

    def grad_copy(n, part):
        source, target = ((part_in, sums_in_ref), (part_out, sums_out_ref))[n]
        if part == 0:
            return pltpu.make_async_copy(source.at[0], target.at[0], g_recv_sem.at[n, 0])
        return pltpu.make_async_remote_copy(
            src_ref=source.at[part],
            dst_ref=target.at[parts - part],
            send_sem=g_send_sem.at[n, part],
            recv_sem=g_recv_sem.at[n, parts - part],
            device_id={"dp": (my_dp + part) % parts},
            device_id_type=MESH,
        )

    for part in list(range(1, parts)) + [0]:
        for n, (left, right, target) in enumerate(
            ((rows_x, d_pre, part_in), (rows_dy, active, part_out))
        ):

            def grads(t, carry, left=left, right=right, target=target, part=part):
                columns = pl.ds(pl.multiple_of(t * tile, tile), tile)
                target[part, columns] = contract_first(left[:, columns], right[part]).astype(BF)
                return carry

            lax.fori_loop(0, width // tile, grads, 0)
            grad_copy(n, part).start()

    totals = None
    for step in order:
        group = paired(my_group, step)
        chosen = jnp.concatenate([selector(group, block) for block in range(4)], axis=0)
        lane = lanes(tok_rows, size * line) + group * size * line
        from_lines = jnp.concatenate((ones_at(lane == line_0), ones_at(lane == line_1)), axis=0)
        await_group(back_gate, back_gate_sem, group, line)
        await_group(back_buf, back_sem, group, chunk)
        terms = [matmul(chosen, back_buf[group]), matmul(from_lines, back_gate[group])]
        totals = terms if totals is None else [a + b for a, b in zip(totals, terms)]
    for block in range(4):
        d_tokens_ref[:, block * quarter : (block + 1) * quarter] = totals[0][
            block * tok_rows : (block + 1) * tok_rows
        ].astype(BF)
    first_gate = jnp.sum(jnp.where(named == slot_0, totals[1][:tok_rows], 0.0), axis=1, keepdims=True)
    second_gate = jnp.sum(jnp.where(named == slot_1, totals[1][tok_rows:], 0.0), axis=1, keepdims=True)
    gate_grad_ref[0:1] = row(first_gate / gate_0).astype(BF)
    gate_grad_ref[1:2] = row(second_gate / gate_1).astype(BF)

    for step in range(GROUPS):
        group = paired(my_group, step)
        for turn in range(size):
            if step or turn:
                member = (my_member + turn) % size
                dispatch_copy(group, member).wait_send()
                return_copy(group, member).wait_send()
                gate_copy(group, member).wait_send()
    for turn in range(1, parts):
        for n, source in enumerate((w_in_ref, w_out_ref)):
            block = source.at[0]
            pltpu.make_async_copy(block, block, w_send_sem.at[n, turn]).wait()
            grad_copy(n, turn).wait_send()
    for part in range(parts):
        for n, target in enumerate((sums_in_ref, sums_out_ref)):
            block = target.at[part]
            pltpu.make_async_copy(block, block, g_recv_sem.at[n, part]).wait()


def stay(array):
    return pltpu.with_memory_space_constraint(array, pltpu.HBM)


def shards(experts, parts, tokens, out_grad, gates, expert_ids, w_in, w_out):
    tok_rows, width = tokens.shape
    hidden = w_in.shape[2]
    cap = 3 * tok_rows // experts
    chunk = -(-4 * cap // 16) * 16
    span = experts // GROUPS * chunk
    slots = experts // GROUPS * cap
    vmem = pl.BlockSpec(memory_space=pltpu.VMEM)
    hbm = pl.BlockSpec(memory_space=pltpu.HBM)
    free = pl.BlockSpec(memory_space=pl.ANY)
    dma = pltpu.SemaphoreType.DMA
    d_tokens, gate_grad, sums_in, sums_out = pl.pallas_call(
        functools.partial(kernel, experts, parts, cap, chunk),
        out_shape=(
            jax.ShapeDtypeStruct((tok_rows, width), BF),
            jax.ShapeDtypeStruct((2, tok_rows), BF),
            jax.ShapeDtypeStruct((parts, width, hidden), BF),
            jax.ShapeDtypeStruct((parts, width, hidden), BF),
        ),
        in_specs=[hbm, hbm, vmem, vmem, hbm, hbm],
        out_specs=(vmem, vmem, free, free),
        scratch_shapes=[
            pltpu.VMEM((4 * tok_rows, width // 2), BF),
            pltpu.VMEM((GROUPS, span, width // 2), BF),
            pltpu.VMEM((GROUPS, span, width // 2), BF),
            pltpu.VMEM((GROUPS, span, width // 4), BF),
            pltpu.VMEM((GROUPS, span, width // 4), BF),
            pltpu.VMEM((GROUPS, experts // GROUPS * 16, 128), BF),
            pltpu.VMEM((GROUPS, experts // GROUPS * 16, 128), BF),
            pltpu.VMEM((4 * slots, span), BF),
            pltpu.VMEM((parts, width, hidden), BF),
            pltpu.VMEM((parts, width, hidden), BF),
            pltpu.VMEM((GROUPS * slots, width), BF),
            pltpu.VMEM((GROUPS * slots, width), BF),
            pltpu.VMEM((parts, GROUPS * slots, hidden), BF),
            pltpu.VMEM((parts, GROUPS * slots, hidden), BF),
            pltpu.VMEM((parts, width, hidden), BF),
            pltpu.VMEM((parts, width, hidden), BF),
            dma((experts,)),
            dma((experts,)),
            dma((experts,)),
            dma((experts,)),
            dma((experts,)),
            dma((experts,)),
            dma((2, parts)),
            dma((2, parts)),
            dma((2, parts)),
            dma((2, parts)),
            dma((4,)),
        ],
        compiler_params=pltpu.CompilerParams(
            collective_id=0, has_side_effects=True, vmem_limit_bytes=36 * 1024 * 1024
        ),
        cost_estimate=pl.CostEstimate(
            flops=10 * GROUPS * slots * width * width,
            bytes_accessed=16 * width * width,
            transcendentals=GROUPS * slots * width,
        ),
    )(
        *map(stay, (tokens, out_grad, gates.T, expert_ids.T, w_in, w_out))
    )
    return (
        d_tokens,
        gate_grad.T,
        jnp.sum(sums_in.astype(F32), axis=0)[None],
        jnp.sum(sums_out.astype(F32), axis=0)[None],
    )


def solution(mesh):
    split = P(("dp", "expert"), None)
    weights = P("expert", None, "dp")
    return jax.shard_map(
        functools.partial(shards, mesh.shape["expert"], mesh.shape["dp"]),
        mesh=mesh,
        in_specs=(split, split, split, split, weights, weights),
        out_specs=(split, split, weights, weights),
        check_vma=False,
    )
```
